512 devices in a mesh: grp: 8 (over z_lo, core), shard: 64 (over z_hi, y, x).
Axes of the slice: x: 4, y: 4, z: 16 (z_hi: 4, z_lo: 4; z = z_hi * 4 + z_lo), core: 2. Of those that a mesh axis runs over, the one named last changes fastest.
Arguments:
- out_param: float32 [8, 256, 16384], P('grp', 'shard'), may hold values from -0.12 to 0.12
- out_grad: bfloat16 [8, 256, 16384], P('grp', 'shard'), may hold values from -2000 to 2000
- out_first: float32 [8, 256, 16384], P('grp', 'shard'), may hold values from -50 to 50
- out_second: float32 [8, 256, 16384], P('grp', 'shard'), may hold values from 0 to 6200
- pair_param: float32 [8, 256, 2048], P('grp', 'shard'), may hold values from -0.12 to 0.12
- pair_grad: bfloat16 [8, 256, 2048], P('grp', 'shard'), may hold values from -2000 to 2000
- pair_first: float32 [8, 256, 2048], P('grp', 'shard'), may hold values from -50 to 50
- pair_second: float32 [8, 256, 2048], P('grp', 'shard'), may hold values from 0 to 6200
Outputs:
- updated_out: float32 [8, 256, 16384], P('grp', 'shard')
- first_out: float32 [8, 256, 16384], P('grp', 'shard')
- second_out: float32 [8, 256, 16384], P('grp', 'shard')
- serving_out: bfloat16 [8, 256, 16384], P(None, None, 'shard')
- updated_pair: float32 [8, 256, 2048], P('grp', 'shard')
- first_pair: float32 [8, 256, 2048], P('grp', 'shard')
- second_pair: float32 [8, 256, 2048], P('grp', 'shard')
- serving_pair: bfloat16 [8, 256, 16384], P(None, None, 'shard')
The draws below stay inside these ranges and needn't reach their ends.
All inputs are finite; a program needn't handle non-finite values.
Results may differ from the reference program's by a relative error of at most 0.001.
Values may be sent and summed in bfloat16 or wider, within the bound.
No kernel may reach another device: no remote copies, remote signals or barrier semaphores. Data moves between devices by JAX's collectives and lax.ppermute only.
A program may use at most 64 MiB of HBM per device.

```python
import math
import jax
import jax.numpy as jnp
from jax import lax

KV_HEADS = 8
HD = 128
HW = 16384
KVW = 1024
COPIES = 8
ROWS = 256
LAYERS = 8


def scale_field(key, columns, salt, growth):
    key = jax.random.fold_in(key, salt)
    key_col, key_row, key_elem = jax.random.split(key, 3)
    shape_full = (LAYERS, ROWS, columns)
    layer_index = lax.broadcasted_iota(jnp.int32, shape_full, 0).astype(jnp.float32)
    row_index = lax.broadcasted_iota(jnp.int32, shape_full, 1).astype(jnp.float32)
    position = (layer_index * ROWS + row_index) / max(LAYERS * ROWS - 1, 1)
    rising = 2.0 * jnp.power(jnp.float32(growth), position)
    column_scale = 10.0 ** jax.random.uniform(key_col, (columns,), jnp.float32, 0.0, 2.0)
    row_scale = 10.0 ** jax.random.uniform(key_row, (LAYERS, ROWS, 1), jnp.float32, 0.0, 1.0)
    element_scale = jnp.exp(1.5 * jnp.clip(jax.random.normal(key_elem, shape_full, jnp.float32), -3.0, 3.0))
    rising_rms = math.sqrt(2.0 * (growth * growth - 1.0) / math.log(growth))
    divisor = rising_rms * 4.637 * 32.95 * 7.48
    return rising * row_scale * column_scale * element_scale / divisor


def make_grad(key, shared, amplitude_shown):
    shape_full = shared.shape
    noise = jnp.clip(jax.random.normal(key, shape_full, jnp.float32), -4.0, 4.0)
    amplitude = amplitude_shown
    return (amplitude * noise * shared).astype(jnp.bfloat16)


def draw_out_grad(key, part):
    growth = 3.0
    shared = scale_field(key, HW, 101, growth)
    key = jax.random.fold_in(key, 11)
    return make_grad(key, shared, 3.49)


def draw_pair_grad(key, part):
    growth = 3.0
    shared = scale_field(key, 2 * KVW, 202, growth)
    key = jax.random.fold_in(key, 23)
    return make_grad(key, shared, 3.49)


def draw_out_first(key, part):
    growth = 3.0
    shared = scale_field(key, HW, 101, growth)
    key = jax.random.fold_in(key, 13)
    noise = jnp.clip(jax.random.normal(key, shared.shape, jnp.float32), -4.0, 4.0)
    return 0.075 * noise * shared


def draw_pair_first(key, part):
    growth = 3.0
    shared = scale_field(key, 2 * KVW, 202, growth)
    key = jax.random.fold_in(key, 29)
    noise = jnp.clip(jax.random.normal(key, shared.shape, jnp.float32), -4.0, 4.0)
    return 0.075 * noise * shared


def draw_out_second(key, part):
    growth = 3.0
    shared = scale_field(key, HW, 101, growth)
    key = jax.random.fold_in(key, 17)
    spread = 10.0 ** jax.random.uniform(key, shared.shape, jnp.float32, -2.0, -1.0)
    return 2.25 * shared * shared * spread


def draw_pair_second(key, part):
    growth = 3.0
    shared = scale_field(key, 2 * KVW, 202, growth)
    key = jax.random.fold_in(key, 31)
    spread = 10.0 ** jax.random.uniform(key, shared.shape, jnp.float32, -2.0, -1.0)
    return 2.25 * shared * shared * spread


def level_of(stream_key, shape, cuts, least, high):
    level = 1.0
    for axis_at, parts in cuts:
        draws = jax.random.uniform(jax.random.fold_in(jax.random.fold_in(stream_key, 6), axis_at), (parts,), jnp.float32, least / len(cuts), high / len(cuts))
        level = level * jnp.repeat(jnp.exp(draws), shape[axis_at] // parts).reshape((-1,) + (1,) * (len(shape) - 1 - axis_at))
    return level


def scatter_about(rng, extent, scale, most, cuts=(), dtype=jnp.bfloat16):
    values = scale * jax.random.normal(rng, extent, jnp.float32)
    if cuts:
        values = values * level_of(rng, extent, cuts, -0.22, 0.18)
    return jnp.clip(values, -most, most).astype(dtype)


def setup_inputs(seed: int = 0) -> dict:
    key_of = jax.random.split(jax.random.key(seed), 9)
    out_param = scatter_about(key_of[0], (LAYERS, ROWS, HW), 0.02, 0.12, ((0, 8), (1, 64)), jnp.float32)
    out_grad = draw_out_grad(jax.random.fold_in(key_of[8], 71), 0)
    out_first = draw_out_first(jax.random.fold_in(key_of[8], 71), 0)
    out_second = draw_out_second(jax.random.fold_in(key_of[8], 71), 0)
    pair_param = scatter_about(key_of[4], (LAYERS, ROWS, 2 * KVW), 0.02, 0.12, ((0, 8), (1, 64)), jnp.float32)
    pair_grad = draw_pair_grad(jax.random.fold_in(key_of[8], 71), 0)
    pair_first = draw_pair_first(jax.random.fold_in(key_of[8], 71), 0)
    pair_second = draw_pair_second(jax.random.fold_in(key_of[8], 71), 0)
    return dict(out_param=out_param, out_grad=out_grad, out_first=out_first, out_second=out_second, pair_param=pair_param, pair_grad=pair_grad, pair_first=pair_first, pair_second=pair_second)


def apply_update(param, gradient, first, second, factor):
    scaled = gradient.astype(jnp.float32) * factor
    first_new = 0.9 * first + 0.1 * scaled
    second_new = 0.95 * second + 0.05 * scaled * scaled
    corr_first = 1.0 - 0.9 ** 20
    corr_second = 1.0 - 0.95 ** 20
    step_size = first_new / corr_first / (jnp.sqrt(second_new / corr_second) + 1e-08)
    param_new = param - 0.001 * (step_size + 0.1 * param)
    return (param_new, first_new, second_new, param_new.astype(jnp.bfloat16))

def head_layout(pair_narrow, copy_count):
    layer_count, row_count, column_count = pair_narrow.shape
    split_heads = pair_narrow.reshape(layer_count, row_count, 2, KV_HEADS, HD)
    by_head = jnp.transpose(split_heads, (0, 1, 3, 2, 4)).reshape(layer_count, row_count, KV_HEADS, 2 * HD)
    copied = jnp.broadcast_to(by_head[:, :, :, None, :], (layer_count, row_count, KV_HEADS, copy_count, 2 * HD))
    return copied.reshape(layer_count, row_count, KV_HEADS * copy_count * 2 * HD)

def reference(out_param, out_grad, out_first, out_second, pair_param, pair_grad, pair_first, pair_second):
    out_wide = out_grad.astype(jnp.float32)
    pair_wide = pair_grad.astype(jnp.float32)
    summed = jnp.sum(out_wide * out_wide) + jnp.sum(pair_wide * pair_wide)
    count = out_grad.size + pair_grad.size
    factor = jnp.minimum(1.0, 1.5 * jnp.sqrt(jnp.float32(count)) / jnp.sqrt(summed))
    out_res = apply_update(out_param, out_grad, out_first, out_second, factor)
    pair_res = apply_update(pair_param, pair_grad, pair_first, pair_second, factor)
    serving_pair = head_layout(pair_res[3], COPIES)
    return (out_res[0], out_res[1], out_res[2], out_res[3], pair_res[0], pair_res[1], pair_res[2], serving_pair)
```

```python
import numpy as np
import jax
import jax.numpy as jnp
from jax import lax
from jax.experimental import pallas as pl
from jax.experimental.pallas import tpu as pltpu
from jax.sharding import Mesh
from jax.sharding import PartitionSpec as P

KV_HEADS = 8
HD = 128
GROUP = ("zl", "core")
SHARD = ("zh", "y", "x")
RING = ("zh", "zl", "core")
PLANE = ("y", "x")


def apply_update(param, gradient, first, second, factor):
    scaled = gradient.astype(jnp.float32) * factor
    first_new = 0.9 * first + 0.1 * scaled
    second_new = 0.95 * second + 0.05 * scaled * scaled
    corr_first = 1.0 - 0.9**20
    corr_second = 1.0 - 0.95**20
    step_size = first_new / corr_first / (jnp.sqrt(second_new / corr_second) + 1e-08)
    param_new = param - 0.001 * (step_size + 0.1 * param)
    return (param_new, first_new, second_new, param_new.astype(jnp.bfloat16))


def total_over(value, axes):
    members = lax.axis_size(axes)
    copies = jnp.broadcast_to(value.reshape(1, 1, 1), (members, 1, 128))
    received = lax.all_to_all(copies, axes, split_axis=0, concat_axis=0, tiled=True)
    return jnp.sum(received[:, 0, 0])


def place_kernel(where_ref, *refs):
    blocks, (out_ref, pair_ref), sems = refs[:8], refs[8:10], refs[10]
    copies = []
    for i in range(8):
        layer = where_ref[i]
        copies.append(pltpu.make_async_copy(blocks[i].at[0], out_ref.at[layer], sems.at[i, 0]))
        copies.append(pltpu.make_async_copy(blocks[i].at[1], pair_ref.at[layer], sems.at[i, 1]))
    for copy in copies:
        copy.start()
    for copy in copies:
        copy.wait()


def place(where, blocks):
    _, rows, columns = blocks[0].shape
    shape = jax.ShapeDtypeStruct((8, rows, columns), jnp.bfloat16)
    anywhere, held = pl.BlockSpec(memory_space=pl.ANY), pl.BlockSpec(memory_space=pltpu.VMEM)
    return pl.pallas_call(
        place_kernel,
        out_shape=(shape, shape),
        in_specs=[pl.BlockSpec(memory_space=pltpu.SMEM)] + [held] * 8,
        out_specs=(anywhere, anywhere),
        scratch_shapes=[pltpu.SemaphoreType.DMA((8, 2))],
    )(where, *blocks)


def per_device(
    out_param, out_grad, out_first, out_second, pair_param, pair_grad, pair_first, pair_second
):
    out_wide = out_grad.astype(jnp.float32)
    pair_wide = pair_grad.astype(jnp.float32)
    local_squares = jnp.sum(out_wide * out_wide) + jnp.sum(pair_wide * pair_wide)
    summed = total_over(total_over(local_squares, RING), PLANE)
    groups, shards = lax.axis_size(GROUP), lax.axis_size(SHARD)
    count = groups * shards * (out_grad.size + pair_grad.size)
    factor = jnp.minimum(1.0, 1.5 * jnp.sqrt(jnp.float32(count)) / jnp.sqrt(summed))
    out_res = apply_update(out_param, out_grad, out_first, out_second, factor)
    pair_res = apply_update(pair_param, pair_grad, pair_first, pair_second, factor)

    rows = out_param.shape[1]
    width = out_param.shape[2] // shards
    out_blocks = jnp.transpose(out_res[3].reshape(rows, shards, width), (1, 0, 2))
    by_head = jnp.transpose(pair_res[3].reshape(rows, 2, KV_HEADS, HD), (2, 0, 1, 3))
    by_head = by_head.reshape(KV_HEADS, 1, rows, 2 * HD)
    pair_blocks = jnp.broadcast_to(by_head, (KV_HEADS, shards // KV_HEADS, rows, 2 * HD))
    pair_blocks = pair_blocks.reshape(shards, rows, 2 * HD)
    sent = jnp.stack([out_blocks, pair_blocks], axis=1)
    mine = lax.all_to_all(sent, SHARD, split_axis=0, concat_axis=0, tiled=True)
    mine = jnp.transpose(mine, (1, 0, 2, 3)).reshape(2, shards * rows, width)

    zl, core = lax.axis_index("zl"), lax.axis_index("core")
    blocks, where = [mine], [2 * zl + core]
    for k in range(1, 4):
        blocks.append(lax.ppermute(mine, "zl", [(i, i ^ k) for i in range(4)]))
        where.append(2 * (zl ^ k) + core)
    for k in range(4):
        blocks.append(lax.ppermute(blocks[k], "core", [(0, 1), (1, 0)]))
        where.append(2 * (zl ^ k) + (1 - core))
    serving = place(jnp.stack(where).astype(jnp.int32), blocks)
    return (
        out_res[0],
        out_res[1],
        out_res[2],
        serving[0],
        pair_res[0],
        pair_res[1],
        pair_res[2],
        serving[1],
    )


def solution(mesh):
    fine = Mesh(mesh.devices.reshape(4, 2, 4, 4, 4), ("zl", "core", "zh", "y", "x"))
    owned = P(GROUP, SHARD, None)
    served = P(None, None, SHARD)
    return jax.shard_map(
        per_device,
        mesh=fine,
        in_specs=(owned,) * 8,
        out_specs=(owned, owned, owned, served, owned, owned, owned, served),
        check_vma=False,
    )
```

```python
import jax
import jax.numpy as jnp
from jax import lax
from jax.experimental import pallas as pl
from jax.experimental.pallas import tpu as pltpu
from jax.sharding import Mesh
from jax.sharding import PartitionSpec as P

KV_HEADS = 8
HD = 128
LANES = 128
GROUP = ("zl", "core")
SHARD = ("zh", "y", "x")
RING = ("zh", "zl", "core")
PLANE = ("y", "x")
TURNS = (0, 2, 1, 3)
VMEM = pl.BlockSpec(memory_space=pltpu.VMEM)
ANY = pl.BlockSpec(memory_space=pl.ANY)
WIDE = pltpu.CompilerParams(vmem_limit_bytes=60 * 1024 * 1024)
SLIM = pltpu.CompilerParams(vmem_limit_bytes=8 * 1024 * 1024)


def apply_update(param, gradient, first, second, factor):
    scaled = gradient.astype(jnp.float32) * factor
    first_new = 0.9 * first + 0.1 * scaled
    second_new = 0.95 * second + 0.05 * scaled * scaled
    corr_first = 1.0 - 0.9**20
    corr_second = 1.0 - 0.95**20
    step_size = first_new / corr_first / (jnp.sqrt(second_new / corr_second) + 1e-08)
    param_new = param - 0.001 * (step_size + 0.1 * param)
    return (param_new, first_new, second_new)


def squares_kernel(out_ref, pair_ref, sums_ref):
    total = jnp.zeros((4, LANES), jnp.float32)
    for ref in (pair_ref, out_ref):
        for at in range(0, ref.shape[2], LANES):
            wide = ref[0, :, at : at + LANES].astype(jnp.float32)
            total = total + wide * wide
    row = jnp.sum(total, axis=0, keepdims=True)
    sums_ref[...] = jnp.broadcast_to(row[None], sums_ref.shape)


def add_kernel(got_ref, sums_ref):
    sums_ref[...] = jnp.broadcast_to(jnp.sum(got_ref[...], axis=0, keepdims=True), sums_ref.shape)


def send_kernel(count, *refs):
    got_ref, out_refs, pair_refs, (sent_ref, factor_ref) = refs[0], refs[1:5], refs[5:9], refs[9:]
    summed = jnp.sum(jnp.sum(got_ref[...], axis=0), keepdims=True)
    factor = jnp.minimum(1.0, 1.5 * jnp.sqrt(jnp.float32(count)) / jnp.sqrt(summed))
    factor_ref[...] = factor

    def narrow(refs, at, size):
        param, grad, first, second = [ref[0, :, at : at + size] for ref in refs]
        return apply_update(param, grad, first, second, factor)[0].astype(jnp.bfloat16)

    shards, _, _, width = sent_ref.shape
    for s in range(shards):
        sent_ref[s, 0] = narrow(out_refs, s * width, width)
    copies = shards // KV_HEADS
    for h in range(KV_HEADS):
        key = narrow(pair_refs, h * HD, HD)
        value = narrow(pair_refs, (KV_HEADS + h) * HD, HD)
        for s in range(h * copies, (h + 1) * copies):
            sent_ref[s, 1, :, :HD] = key
            sent_ref[s, 1, :, HD:] = value


def state_kernel(*refs):
    factor = refs[0][...]
    for given, made in ((refs[1:5], refs[9:12]), (refs[5:9], refs[12:15])):
        size = min(given[0].shape[2], 1024)
        for at in range(0, given[0].shape[2], size):
            values = apply_update(*[ref[0, :, at : at + size] for ref in given], factor)
            for ref, value in zip(made, values):
                ref[0, :, at : at + size] = value


def place_kernel(*refs):
    blocks, out_ref, pair_ref, sems = refs[:8], refs[8], refs[9], refs[10]
    zl, core = lax.axis_index("zl"), lax.axis_index("core")
    copies = []
    for i, ref in enumerate(blocks):
        layer = 2 * (zl ^ TURNS[i % 4]) + (core if i < 4 else 1 - core)
        copies.append(pltpu.make_async_copy(ref.at[0], out_ref.at[layer], sems.at[i, 0]))
        copies.append(pltpu.make_async_copy(ref.at[1], pair_ref.at[layer], sems.at[i, 1]))
    for copy in copies:
        copy.start()
    for copy in copies:
        copy.wait()


def swap(value, axes):
    return lax.all_to_all(value, axes, split_axis=0, concat_axis=0, tiled=True)


def per_device(*given):
    groups, shards = lax.axis_size(GROUP), lax.axis_size(SHARD)
    devices = groups * shards
    count = devices * (given[1].size + given[5].size)
    rows = given[0].shape[1]
    width = given[0].shape[2] // shards

    def sums(axes):
        return jax.ShapeDtypeStruct((lax.axis_size(axes), 1, LANES), jnp.float32)

    squares = pl.pallas_call(
        squares_kernel, out_shape=sums(RING), in_specs=[VMEM] * 2, out_specs=VMEM,
        compiler_params=WIDE,
    )(given[1], given[5])
    ring_sums = pl.pallas_call(
        add_kernel, out_shape=sums(PLANE), in_specs=[VMEM], out_specs=VMEM,
        compiler_params=SLIM,
    )(swap(squares, RING))
    plane_sums = swap(ring_sums, PLANE)
    sent, factor = pl.pallas_call(
        lambda *refs: send_kernel(count, *refs),
        out_shape=(
            jax.ShapeDtypeStruct((shards, 2, rows, width), jnp.bfloat16),
            jax.ShapeDtypeStruct((1, 1), jnp.float32),
        ),
        in_specs=[VMEM] * 9,
        out_specs=(VMEM, VMEM),
        compiler_params=WIDE,
    )(plane_sums, *given)
    mine = swap(sent, SHARD)

    mine, factor = lax.optimization_barrier((mine, factor))
    state = pl.pallas_call(
        state_kernel,
        out_shape=[
            jax.ShapeDtypeStruct(given[i].shape, jnp.float32) for i in (0, 0, 0, 4, 4, 4)
        ],
        in_specs=[VMEM] * 9,
        out_specs=[VMEM] * 6,
        compiler_params=WIDE,
        cost_estimate=pl.CostEstimate(
            flops=20 * count // devices, bytes_accessed=26 * count // devices, transcendentals=0
        ),
    )(factor, *given)

    mine = jnp.transpose(mine, (1, 0, 2, 3)).reshape(2, shards * rows, width)
    near = [mine]
    for k in TURNS[1:]:
        near.append(lax.ppermute(mine, "zl", [(i, i ^ k) for i in range(4)]))
    near[0], state = lax.optimization_barrier((near[0], state))
    far = [lax.ppermute(block, "core", [(0, 1), (1, 0)]) for block in near]
    serving_shape = jax.ShapeDtypeStruct((groups, shards * rows, width), jnp.bfloat16)
    serving = pl.pallas_call(
        place_kernel,
        out_shape=(serving_shape, serving_shape),
        in_specs=[ANY] * 8,
        out_specs=(ANY, ANY),
        scratch_shapes=[pltpu.SemaphoreType.DMA((8, 2))],
        compiler_params=SLIM,
    )(*near, *far)
    return (*state[:3], serving[0], *state[3:], serving[1])


def solution(mesh):
    fine = Mesh(mesh.devices.reshape(4, 2, 4, 4, 4), ("zl", "core", "zh", "y", "x"))
    owned = P(GROUP, SHARD, None)
    served = P(None, None, SHARD)
    return jax.shard_map(
        per_device,
        mesh=fine,
        in_specs=(owned,) * 8,
        out_specs=(owned, owned, owned, served, owned, owned, owned, served),
        check_vma=False,
    )
```

```python
import jax
import jax.numpy as jnp
from jax import lax
from jax.experimental import pallas as pl
from jax.experimental.pallas import tpu as pltpu
from jax.sharding import Mesh
from jax.sharding import PartitionSpec as P

KV_HEADS = 8
HD = 128
LANES = 128
GRADS = (1, 5)
GROUP = ("zl", "core")
SHARD = ("zh", "y", "x")
RING = ("zh", "zl", "core")
PLANE = ("y", "x")
TURNS = (0, 2, 1, 3)
VMEM = pl.BlockSpec(memory_space=pltpu.VMEM)
ANY = pl.BlockSpec(memory_space=pl.ANY)
HBM = pl.BlockSpec(memory_space=pltpu.HBM)
SLIM = pltpu.CompilerParams(vmem_limit_bytes=8 * 1024 * 1024)


def apply_update(param, gradient, first, second, factor):
    scaled = gradient.astype(jnp.float32) * factor
    first_new = 0.9 * first + 0.1 * scaled
    second_new = 0.95 * second + 0.05 * scaled * scaled
    corr_first = 1.0 - 0.9**20
    corr_second = 1.0 - 0.95**20
    step_size = first_new / corr_first / (jnp.sqrt(second_new / corr_second) + 1e-08)
    param_new = param - 0.001 * (step_size + 0.1 * param)
    return (param_new, first_new, second_new)


def load_kernel(*refs):
    given, held, sums_ref, sems = refs[:8], refs[8:16], refs[16], refs[17]
    order = GRADS + tuple(i for i in range(8) if i not in GRADS)
    copies = {i: pltpu.make_async_copy(given[i], held[i], sems.at[i]) for i in order}
    for i in order:
        copies[i].start()
    total = jnp.zeros((4, LANES), jnp.float32)
    for i in GRADS:
        copies[i].wait()
    for i in GRADS:
        for at in range(0, held[i].shape[2], LANES):
            wide = held[i][0, :, at : at + LANES].astype(jnp.float32)
            total = total + wide * wide
    row = jnp.sum(total, axis=0, keepdims=True)
    sums_ref[...] = jnp.broadcast_to(row[None], sums_ref.shape)
    for i in order[2:]:
        copies[i].wait()


def add_kernel(got_ref, sums_ref):
    sums_ref[...] = jnp.broadcast_to(jnp.sum(got_ref[...], axis=0, keepdims=True), sums_ref.shape)


def send_kernel(count, *refs):
    got_ref, out_refs, pair_refs, (sent_ref, factor_ref) = refs[0], refs[1:5], refs[5:9], refs[9:]
    summed = jnp.sum(jnp.sum(got_ref[...], axis=0), keepdims=True)
    factor = jnp.minimum(1.0, 1.5 * jnp.sqrt(jnp.float32(count)) / jnp.sqrt(summed))
    factor_ref[...] = factor

    def narrow(refs, at, size):
        param, grad, first, second = [ref[0, :, at : at + size] for ref in refs]
        return apply_update(param, grad, first, second, factor)[0].astype(jnp.bfloat16)

    shards, _, _, width = sent_ref.shape
    for s in range(shards):
        sent_ref[s, 0] = narrow(out_refs, s * width, width)
    copies = shards // KV_HEADS
    for h in range(KV_HEADS):
        key = narrow(pair_refs, h * HD, HD)
        value = narrow(pair_refs, (KV_HEADS + h) * HD, HD)
        for s in range(h * copies, (h + 1) * copies):
            sent_ref[s, 1, :, :HD] = key
            sent_ref[s, 1, :, HD:] = value


def state_kernel(*refs):
    factor = refs[0][...]
    for given, made in ((refs[1:5], refs[9:12]), (refs[5:9], refs[12:15])):
        size = min(given[0].shape[2], 1024)
        for at in range(0, given[0].shape[2], size):
            values = apply_update(*[ref[0, :, at : at + size] for ref in given], factor)
            for ref, value in zip(made, values):
                ref[0, :, at : at + size] = value


def place_kernel(*refs):
    blocks, out_ref, pair_ref, sems = refs[:8], refs[8], refs[9], refs[10]
    zl, core = lax.axis_index("zl"), lax.axis_index("core")
    copies = []
    for i, ref in enumerate(blocks):
        layer = 2 * (zl ^ TURNS[i % 4]) + (core if i < 4 else 1 - core)
        copies.append(pltpu.make_async_copy(ref.at[0], out_ref.at[layer], sems.at[i, 0]))
        copies.append(pltpu.make_async_copy(ref.at[1], pair_ref.at[layer], sems.at[i, 1]))
    for copy in copies:
        copy.start()
    for copy in copies:
        copy.wait()


def swap(value, axes):
    return lax.all_to_all(value, axes, split_axis=0, concat_axis=0, tiled=True)


def per_device(*given):
    groups, shards = lax.axis_size(GROUP), lax.axis_size(SHARD)
    devices = groups * shards
    count = devices * (given[1].size + given[5].size)
    rows = given[0].shape[1]
    width = given[0].shape[2] // shards

    def sums(axes):
        return jax.ShapeDtypeStruct((lax.axis_size(axes), 1, LANES), jnp.float32)

    *held, squares = pl.pallas_call(
        load_kernel,
        out_shape=[jax.ShapeDtypeStruct(x.shape, x.dtype) for x in given] + [sums(RING)],
        in_specs=[HBM] * 8,
        out_specs=[VMEM] * 9,
        scratch_shapes=[pltpu.SemaphoreType.DMA((8,))],
        compiler_params=SLIM,
    )(*[pltpu.with_memory_space_constraint(x, pltpu.HBM) for x in given])
    ring_sums = pl.pallas_call(
        add_kernel, out_shape=sums(PLANE), in_specs=[VMEM], out_specs=VMEM,
        compiler_params=SLIM,
    )(swap(squares, RING))
    plane_sums = swap(ring_sums, PLANE)
    sent, factor = pl.pallas_call(
        lambda *refs: send_kernel(count, *refs),
        out_shape=(
            jax.ShapeDtypeStruct((shards, 2, rows, width), jnp.bfloat16),
            jax.ShapeDtypeStruct((1, 1), jnp.float32),
        ),
        in_specs=[VMEM] * 9,
        out_specs=(VMEM, VMEM),
        compiler_params=SLIM,
    )(plane_sums, *held)
    mine = swap(sent, SHARD)

    mine, factor = lax.optimization_barrier((mine, factor))
    state = pl.pallas_call(
        state_kernel,
        out_shape=[
            jax.ShapeDtypeStruct(given[i].shape, jnp.float32) for i in (0, 0, 0, 4, 4, 4)
        ],
        in_specs=[VMEM] * 9,
        out_specs=[VMEM] * 6,
        compiler_params=SLIM,
        cost_estimate=pl.CostEstimate(
            flops=20 * count // devices, bytes_accessed=26 * count // devices, transcendentals=0
        ),
    )(factor, *held)

    mine = jnp.transpose(mine, (1, 0, 2, 3)).reshape(2, shards * rows, width)
    near = [mine]
    for k in TURNS[1:]:
        near.append(lax.ppermute(mine, "zl", [(i, i ^ k) for i in range(4)]))
    near[0], state = lax.optimization_barrier((near[0], state))
    far = [lax.ppermute(block, "core", [(0, 1), (1, 0)]) for block in near]
    serving_shape = jax.ShapeDtypeStruct((groups, shards * rows, width), jnp.bfloat16)
    serving = pl.pallas_call(
        place_kernel,
        out_shape=(serving_shape, serving_shape),
        in_specs=[ANY] * 8,
        out_specs=(ANY, ANY),
        scratch_shapes=[pltpu.SemaphoreType.DMA((8, 2))],
        compiler_params=SLIM,
    )(*near, *far)
    return (*state[:3], serving[0], *state[3:], serving[1])


def solution(mesh):
    fine = Mesh(mesh.devices.reshape(4, 2, 4, 4, 4), ("zl", "core", "zh", "y", "x"))
    owned = P(GROUP, SHARD, None)
    served = P(None, None, SHARD)
    return jax.shard_map(
        per_device,
        mesh=fine,
        in_specs=(owned,) * 8,
        out_specs=(owned, owned, owned, served, owned, owned, owned, served),
        check_vma=False,
    )
```

```python
import jax
import jax.numpy as jnp
from jax import lax
from jax.experimental import pallas as pl
from jax.experimental.pallas import tpu as pltpu
from jax.sharding import Mesh
from jax.sharding import PartitionSpec as P

KV_HEADS = 8
HD = 128
LANES = 128
GRADS = (1, 5)
GROUP = ("zl", "core")
SHARD = ("zh", "y", "x")
RING = ("zh", "zl", "core")
PLANE = ("y", "x")
TURNS = (0, 2, 1, 3)
VMEM = pl.BlockSpec(memory_space=pltpu.VMEM)
ANY = pl.BlockSpec(memory_space=pl.ANY)
HBM = pl.BlockSpec(memory_space=pltpu.HBM)
SLIM = pltpu.CompilerParams(vmem_limit_bytes=8 * 1024 * 1024)


def apply_update(param, gradient, first, second, factor):
    scaled = gradient.astype(jnp.float32) * factor
    first_new = 0.9 * first + 0.1 * scaled
    second_new = 0.95 * second + 0.05 * scaled * scaled
    corr_first = 1.0 - 0.9**20
    corr_second = 1.0 - 0.95**20
    step_size = first_new / corr_first / (jnp.sqrt(second_new / corr_second) + 1e-08)
    param_new = param - 0.001 * (step_size + 0.1 * param)
    return (param_new, first_new, second_new)


def load_kernel(*refs):
    given, held, sums_ref, sems = refs[:8], refs[8:16], refs[16], refs[17]
    order = GRADS + tuple(i for i in range(8) if i not in GRADS)
    copies = {i: pltpu.make_async_copy(given[i], held[i], sems.at[i]) for i in order}
    for i in order:
        copies[i].start()
    total = jnp.zeros((4, LANES), jnp.float32)
    for i in GRADS:
        copies[i].wait()
    for i in GRADS:
        for at in range(0, held[i].shape[2], LANES):
            wide = held[i][0, :, at : at + LANES].astype(jnp.float32)
            total = total + wide * wide
    row = jnp.sum(total, axis=0, keepdims=True)
    sums_ref[...] = jnp.broadcast_to(row[None], sums_ref.shape)
    for i in order[2:]:
        copies[i].wait()


def add_kernel(got_ref, sums_ref):
    sums_ref[...] = jnp.broadcast_to(jnp.sum(got_ref[...], axis=0, keepdims=True), sums_ref.shape)


def send_kernel(count, *refs):
    got_ref, out_refs, pair_refs, (sent_ref, factor_ref) = refs[0], refs[1:5], refs[5:9], refs[9:]
    summed = jnp.sum(jnp.sum(got_ref[...], axis=0), keepdims=True)
    factor = jnp.minimum(1.0, 1.5 * jnp.sqrt(jnp.float32(count)) / jnp.sqrt(summed))
    factor_ref[...] = factor

    def narrow(refs, at, size):
        param, grad, first, second = [ref[0, :, at : at + size] for ref in refs]
        return apply_update(param, grad, first, second, factor)[0].astype(jnp.bfloat16)

    shards, _, _, width = sent_ref.shape
    for s in range(shards):
        sent_ref[s, 0] = narrow(out_refs, s * width, width)
    copies = shards // KV_HEADS
    for h in range(KV_HEADS):
        key = narrow(pair_refs, h * HD, HD)
        value = narrow(pair_refs, (KV_HEADS + h) * HD, HD)
        for s in range(h * copies, (h + 1) * copies):
            sent_ref[s, 1, :, :HD] = key
            sent_ref[s, 1, :, HD:] = value


def state_kernel(*refs):
    factor = refs[0][...]
    for given, made in ((refs[1:5], refs[9:12]), (refs[5:9], refs[12:15])):
        size = min(given[0].shape[2], 1024)
        for at in range(0, given[0].shape[2], size):
            values = apply_update(*[ref[0, :, at : at + size] for ref in given], factor)
            for ref, value in zip(made, values):
                ref[0, :, at : at + size] = value


def place_kernel(turns, *refs):
    blocks, (out_ref, pair_ref, sems) = refs[: 2 * len(turns)], refs[-3:]
    zl, core = lax.axis_index("zl"), lax.axis_index("core")
    copies = []
    for i, ref in enumerate(blocks):
        layer = 2 * (zl ^ turns[i // 2]) + (1 - core if i % 2 else core)
        copies.append(pltpu.make_async_copy(ref.at[0], out_ref.at[layer], sems.at[i, 0]))
        copies.append(pltpu.make_async_copy(ref.at[1], pair_ref.at[layer], sems.at[i, 1]))
    for copy in copies:
        copy.start()
    for copy in copies:
        copy.wait()


def place(turns, blocks, shape, begun):
    return pl.pallas_call(
        lambda *refs: place_kernel(turns, *refs),
        out_shape=(shape, shape),
        in_specs=[ANY] * (len(blocks) + len(begun)),
        out_specs=(ANY, ANY),
        scratch_shapes=[pltpu.SemaphoreType.DMA((len(blocks), 2))],
        input_output_aliases={len(blocks) + i: i for i in range(len(begun))},
        compiler_params=SLIM,
        cost_estimate=pl.CostEstimate(
            flops=0, bytes_accessed=2 * len(blocks) * 2**18, transcendentals=0
        ),
    )(*blocks, *begun)


def swap(value, axes):
    return lax.all_to_all(value, axes, split_axis=0, concat_axis=0, tiled=True)


def per_device(*given):
    groups, shards = lax.axis_size(GROUP), lax.axis_size(SHARD)
    devices = groups * shards
    count = devices * (given[1].size + given[5].size)
    rows = given[0].shape[1]
    width = given[0].shape[2] // shards

    def sums(axes):
        return jax.ShapeDtypeStruct((lax.axis_size(axes), 1, LANES), jnp.float32)

    *held, squares = pl.pallas_call(
        load_kernel,
        out_shape=[jax.ShapeDtypeStruct(x.shape, x.dtype) for x in given] + [sums(RING)],
        in_specs=[HBM] * 8,
        out_specs=[VMEM] * 9,
        scratch_shapes=[pltpu.SemaphoreType.DMA((8,))],
        compiler_params=SLIM,
    )(*[pltpu.with_memory_space_constraint(x, pltpu.HBM) for x in given])
    ring_sums = pl.pallas_call(
        add_kernel, out_shape=sums(PLANE), in_specs=[VMEM], out_specs=VMEM,
        compiler_params=SLIM,
    )(swap(squares, RING))
    plane_sums = swap(ring_sums, PLANE)
    sent, factor = pl.pallas_call(
        lambda *refs: send_kernel(count, *refs),
        out_shape=(
            jax.ShapeDtypeStruct((shards, 2, rows, width), jnp.bfloat16),
            jax.ShapeDtypeStruct((1, 1), jnp.float32),
        ),
        in_specs=[VMEM] * 9,
        out_specs=(VMEM, VMEM),
        compiler_params=SLIM,
    )(plane_sums, *held)
    mine = swap(sent, SHARD)

    mine, factor = lax.optimization_barrier((mine, factor))
    state = pl.pallas_call(
        state_kernel,
        out_shape=[
            jax.ShapeDtypeStruct(given[i].shape, jnp.float32) for i in (0, 0, 0, 4, 4, 4)
        ],
        in_specs=[VMEM] * 9,
        out_specs=[VMEM] * 6,
        compiler_params=SLIM,
        cost_estimate=pl.CostEstimate(
            flops=20 * count // devices, bytes_accessed=26 * count // devices, transcendentals=0
        ),
    )(factor, *held)

    mine = jnp.transpose(mine, (1, 0, 2, 3)).reshape(2, shards * rows, width)
    near = [mine]
    for k in TURNS[1:]:
        near.append(lax.ppermute(mine, "zl", [(i, i ^ k) for i in range(4)]))
    near[0], state = lax.optimization_barrier((near[0], state))
    far = [lax.ppermute(block, "core", [(0, 1), (1, 0)]) for block in near]
    shape = jax.ShapeDtypeStruct((groups, shards * rows, width), jnp.bfloat16)
    pairs = [(near[i], far[i]) for i in range(4)]
    early = [block for i in (0, 2, 3) for block in pairs[i]]
    begun = place([TURNS[i] for i in (0, 2, 3)], early, shape, ())
    serving = place([TURNS[1]], pairs[1], shape, begun)
    return (*state[:3], serving[0], *state[3:], serving[1])


def solution(mesh):
    fine = Mesh(mesh.devices.reshape(4, 2, 4, 4, 4), ("zl", "core", "zh", "y", "x"))
    owned = P(GROUP, SHARD, None)
    served = P(None, None, SHARD)
    return jax.shard_map(
        per_device,
        mesh=fine,
        in_specs=(owned,) * 8,
        out_specs=(owned, owned, owned, served, owned, owned, owned, served),
        check_vma=False,
    )
```

```python
import jax
import jax.numpy as jnp
from jax import lax
from jax.experimental import pallas as pl
from jax.experimental.pallas import tpu as pltpu
from jax.sharding import Mesh
from jax.sharding import PartitionSpec as P

KV_HEADS = 8
HD = 128
LANES = 128
GRADS = (1, 5)
GROUP = ("zl", "core")
SHARD = ("zh", "y", "x")
RING = ("zh", "zl", "core")
PLANE = ("y", "x")
TURNS = (0, 2, 1, 3)
VMEM = pl.BlockSpec(memory_space=pltpu.VMEM)
ANY = pl.BlockSpec(memory_space=pl.ANY)
HBM = pl.BlockSpec(memory_space=pltpu.HBM)
SLIM = pltpu.CompilerParams(vmem_limit_bytes=8 * 1024 * 1024)


def apply_update(param, gradient, first, second, factor):
    scaled = gradient.astype(jnp.float32) * factor
    first_new = 0.9 * first + 0.1 * scaled
    second_new = 0.95 * second + 0.05 * scaled * scaled
    corr_first = 1.0 - 0.9**20
    corr_second = 1.0 - 0.95**20
    step_size = first_new / corr_first / (jnp.sqrt(second_new / corr_second) + 1e-08)
    param_new = param - 0.001 * (step_size + 0.1 * param)
    return (param_new, first_new, second_new)


def load_kernel(*refs):
    given, held, sums_ref, sems = refs[:8], refs[8:16], refs[16], refs[17]
    order = GRADS + tuple(i for i in range(8) if i not in GRADS)
    copies = {i: pltpu.make_async_copy(given[i], held[i], sems.at[i]) for i in order}
    for i in order:
        copies[i].start()
    totals = [jnp.zeros((4, LANES), jnp.float32) for _ in range(4)]
    for i in reversed(GRADS):
        copies[i].wait()
        for at in range(0, held[i].shape[2], LANES):
            wide = held[i][0, :, at : at + LANES].astype(jnp.float32)
            turn = at // LANES % 4
            totals[turn] = totals[turn] + wide * wide
    total = (totals[0] + totals[1]) + (totals[2] + totals[3])
    row = jnp.sum(total, axis=0, keepdims=True)
    sums_ref[...] = jnp.broadcast_to(row[None], sums_ref.shape)
    for i in order[2:]:
        copies[i].wait()


def add_kernel(got_ref, sums_ref):
    sums_ref[...] = jnp.broadcast_to(jnp.sum(got_ref[...], axis=0, keepdims=True), sums_ref.shape)


def send_kernel(count, *refs):
    got_ref, out_refs, pair_refs, (sent_ref, factor_ref) = refs[0], refs[1:5], refs[5:9], refs[9:]
    summed = jnp.sum(jnp.sum(got_ref[...], axis=0), keepdims=True)
    factor = jnp.minimum(1.0, 1.5 * jnp.sqrt(jnp.float32(count)) / jnp.sqrt(summed))
    factor_ref[...] = factor

    def narrow(refs, at, size):
        param, grad, first, second = [ref[0, :, at : at + size] for ref in refs]
        return apply_update(param, grad, first, second, factor)[0].astype(jnp.bfloat16)

    shards, _, _, width = sent_ref.shape
    for s in range(shards):
        sent_ref[s, 0] = narrow(out_refs, s * width, width)
    copies = shards // KV_HEADS
    for h in range(KV_HEADS):
        key = narrow(pair_refs, h * HD, HD)
        value = narrow(pair_refs, (KV_HEADS + h) * HD, HD)
        for s in range(h * copies, (h + 1) * copies):
            sent_ref[s, 1, :, :HD] = key
            sent_ref[s, 1, :, HD:] = value


def state_kernel(*refs):
    factor = refs[0][...]
    for given, made in ((refs[1:5], refs[9:12]), (refs[5:9], refs[12:15])):
        size = min(given[0].shape[2], 1024)
        for at in range(0, given[0].shape[2], size):
            values = apply_update(*[ref[0, :, at : at + size] for ref in given], factor)
            for ref, value in zip(made, values):
                ref[0, :, at : at + size] = value


def place_kernel(turns, *refs):
    blocks, (out_ref, pair_ref, sems) = refs[: 2 * len(turns)], refs[-3:]
    zl, core = lax.axis_index("zl"), lax.axis_index("core")
    copies = []
    for i, ref in enumerate(blocks):
        layer = 2 * (zl ^ turns[i // 2]) + (1 - core if i % 2 else core)
        copies.append(pltpu.make_async_copy(ref.at[0], out_ref.at[layer], sems.at[i, 0]))
        copies.append(pltpu.make_async_copy(ref.at[1], pair_ref.at[layer], sems.at[i, 1]))
    for i, copy in enumerate(copies):
        copy.start(priority=i % 2)
    for copy in copies:
        copy.wait()


def place(turns, blocks, shape, begun):
    return pl.pallas_call(
        lambda *refs: place_kernel(turns, *refs),
        out_shape=(shape, shape),
        in_specs=[ANY] * (len(blocks) + len(begun)),
        out_specs=(ANY, ANY),
        scratch_shapes=[pltpu.SemaphoreType.DMA((len(blocks), 2))],
        input_output_aliases={len(blocks) + i: i for i in range(len(begun))},
        compiler_params=SLIM,
        cost_estimate=pl.CostEstimate(
            flops=0, bytes_accessed=2 * len(blocks) * 2**18, transcendentals=0
        ),
    )(*blocks, *begun)


def swap(value, axes):
    return lax.all_to_all(value, axes, split_axis=0, concat_axis=0, tiled=True)


def per_device(*given):
    groups, shards = lax.axis_size(GROUP), lax.axis_size(SHARD)
    devices = groups * shards
    count = devices * (given[1].size + given[5].size)
    rows = given[0].shape[1]
    width = given[0].shape[2] // shards

    def sums(axes):
        return jax.ShapeDtypeStruct((lax.axis_size(axes), 1, LANES), jnp.float32)

    *held, squares = pl.pallas_call(
        load_kernel,
        out_shape=[jax.ShapeDtypeStruct(x.shape, x.dtype) for x in given] + [sums(RING)],
        in_specs=[HBM] * 8,
        out_specs=[VMEM] * 9,
        scratch_shapes=[pltpu.SemaphoreType.DMA((8,))],
        compiler_params=SLIM,
    )(*[pltpu.with_memory_space_constraint(x, pltpu.HBM) for x in given])
    ring_sums = pl.pallas_call(
        add_kernel, out_shape=sums(PLANE), in_specs=[VMEM], out_specs=VMEM,
        compiler_params=SLIM,
    )(swap(squares, RING))
    plane_sums = swap(ring_sums, PLANE)
    sent, factor = pl.pallas_call(
        lambda *refs: send_kernel(count, *refs),
        out_shape=(
            jax.ShapeDtypeStruct((shards, 2, rows, width), jnp.bfloat16),
            jax.ShapeDtypeStruct((1, 1), jnp.float32),
        ),
        in_specs=[VMEM] * 9,
        out_specs=(VMEM, VMEM),
        compiler_params=SLIM,
    )(plane_sums, *held)
    mine = swap(sent, SHARD)

    mine, factor = lax.optimization_barrier((mine, factor))
    state = pl.pallas_call(
        state_kernel,
        out_shape=[
            jax.ShapeDtypeStruct(given[i].shape, jnp.float32) for i in (0, 0, 0, 4, 4, 4)
        ],
        in_specs=[VMEM] * 9,
        out_specs=[VMEM] * 6,
        compiler_params=SLIM,
        cost_estimate=pl.CostEstimate(
            flops=20 * count // devices, bytes_accessed=26 * count // devices, transcendentals=0
        ),
    )(factor, *held)

    mine = jnp.transpose(mine, (1, 0, 2, 3)).reshape(2, shards * rows, width)
    near = [mine]
    for k in TURNS[1:]:
        near.append(lax.ppermute(mine, "zl", [(i, i ^ k) for i in range(4)]))
    near[0], state = lax.optimization_barrier((near[0], state))
    far = [lax.ppermute(block, "core", [(0, 1), (1, 0)]) for block in near]
    shape = jax.ShapeDtypeStruct((groups, shards * rows, width), jnp.bfloat16)
    pairs = [(near[i], far[i]) for i in range(4)]
    early = [block for i in (0, 2, 3) for block in pairs[i]]
    begun = place([TURNS[i] for i in (0, 2, 3)], early, shape, ())
    serving = place([TURNS[1]], pairs[1], shape, begun)
    return (*state[:3], serving[0], *state[3:], serving[1])


def solution(mesh):
    fine = Mesh(mesh.devices.reshape(4, 2, 4, 4, 4), ("zl", "core", "zh", "y", "x"))
    owned = P(GROUP, SHARD, None)
    served = P(None, None, SHARD)
    return jax.shard_map(
        per_device,
        mesh=fine,
        in_specs=(owned,) * 8,
        out_specs=(owned, owned, owned, served, owned, owned, owned, served),
        check_vma=False,
    )
```
